32 devices in a mesh: tm: 4 (over y, x), video: 8 (over z, core).
Axes of the slice: x: 2, y: 2, z: 4, core: 2. Of those that a mesh axis runs over, the one named last changes fastest.
Arguments:
- latent: bfloat16 [4, 3, 4, 12, 128, 16], P('tm', None, None, None, 'video'), may hold values from -6 to 6
- routing: int32 [4], replicated, may hold values from 0 to 3, each once
- counts: int32 [4], replicated, may hold values from 1 to 4, as said below
- offsets: int32 [4], replicated, may hold values from 0 to 3, as said below
- in_weight: bfloat16 [3, 3, 48, 384], replicated, may hold values from -0.3125 to 0.3125
- in_bias: float32 [384], replicated, may hold values from -3 to 3
- first_gain: float32 [384], replicated, may hold values from 0.1 to 1.9
- first_weight: bfloat16 [3, 3, 1152, 384], replicated, may hold values from -0.0625 to 0.0625
- first_bias: float32 [384], replicated, may hold values from -3 to 3
- second_gain: float32 [384], replicated, may hold values from 0.1 to 1.9
- second_weight: bfloat16 [3, 3, 1152, 384], replicated, may hold values from -0.0625 to 0.0625
- second_bias: float32 [384], replicated, may hold values from -3 to 3
Outputs:
- decoded: bfloat16 [4, 3, 48, 128, 384], P('tm', None, 'video')
The draws below stay inside these ranges and needn't reach their ends.
Inputs may be any that keep to these rules, and one draw needn't show every extreme that they name: `routing`: a permutation: each video has its own decoder slot. `counts`: every video has at least one span. offsets[v] + counts[v] <= 4.
All inputs are finite; a program needn't handle non-finite values.
Results may differ from the reference program's by a relative error of at most 0.013.
Values may be sent and summed in bfloat16 or wider, within the bound.
A program may use at most 384 MiB of HBM per device.

```python
import jax
import jax.numpy as jnp
from jax import lax

C = 384
Z = 16
ROWS = 3
COLS = 128
FR = 3
BANDS = 4
VPG = 2
SPANS = 4
VIDS = 4
WROWS = 12


def span_plan(key):
    pick_key, spare_key, base_key, late_key = jax.random.split(key, 4)
    full_video = jax.random.randint(pick_key, (), 0, VIDS)
    single = (full_video + 1 + jax.random.randint(spare_key, (), 0, VIDS - 1)) % VIDS
    slot_ids = jnp.arange(VIDS)
    span_counts = jax.random.randint(base_key, (VIDS,), 1, SPANS + 1)
    span_counts = jnp.where(slot_ids == full_video, SPANS, jnp.where(slot_ids == single, 1, span_counts))
    first_slots = jax.random.randint(late_key, (VIDS,), 0, SPANS - span_counts + 1)
    first_slots = jnp.where(slot_ids == single, SPANS - 1, first_slots)
    return (span_counts.astype(jnp.int32), first_slots.astype(jnp.int32))


def draw_counts(key, part):
    return span_plan(key)[0]


def draw_offsets(key, part):
    return span_plan(key)[1]


def steps_of(own_key, extent, shards, smallest, largest):
    loudness = 1.0
    for position, parts in shards:
        draws = jax.random.uniform(jax.random.fold_in(jax.random.fold_in(own_key, 6), position), (parts,), jnp.float32, smallest / len(shards), largest / len(shards))
        loudness = loudness * jnp.repeat(jnp.exp(draws), extent[position] // parts).reshape((-1,) + (1,) * (len(extent) - 1 - position))
    return loudness


def noise(rng, shape, deviation, bound, pieces=(), held_as=jnp.bfloat16):
    entries = deviation * jax.random.normal(rng, shape, jnp.float32)
    if pieces:
        entries = entries * steps_of(rng, shape, pieces, -0.22, 0.18)
    return jnp.clip(entries, -bound, bound).astype(held_as)


def setup_inputs(seed: int = 0) -> dict:
    key_list = jax.random.split(jax.random.key(seed), 13)
    latent = noise(key_list[0], (SPANS, FR, VIDS, WROWS, COLS, Z), 1.0, 6.0, ((0, 4), (4, 8)))
    routing = jax.random.permutation(key_list[1], VIDS).astype(jnp.int32)
    counts = draw_counts(jax.random.fold_in(key_list[12], 71), 0)
    offsets = draw_offsets(jax.random.fold_in(key_list[12], 71), 0)
    in_weight = noise(key_list[4], (3, 3, 3 * Z, C), (27 * Z) ** -0.5, 0.3125)
    in_bias = noise(key_list[5], (C,), 0.5, 3.0, (), jnp.float32)
    first_gain = jnp.clip(1.0 + 0.18 * jax.random.normal(key_list[6], (C,), jnp.float32), 0.1, 1.9)
    first_weight = noise(key_list[7], (3, 3, 3 * C, C), (27 * C) ** -0.5, 0.0625)
    first_bias = noise(key_list[8], (C,), 0.5, 3.0, (), jnp.float32)
    second_gain = jnp.clip(1.0 + 0.18 * jax.random.normal(key_list[9], (C,), jnp.float32), 0.1, 1.9)
    second_weight = noise(key_list[10], (3, 3, 3 * C, C), (27 * C) ** -0.5, 0.0625)
    second_bias = noise(key_list[11], (C,), 0.5, 3.0, (), jnp.float32)
    return dict(latent=latent, routing=routing, counts=counts, offsets=offsets, in_weight=in_weight, in_bias=in_bias, first_gain=first_gain, first_weight=first_weight, first_bias=first_bias, second_gain=second_gain, second_weight=second_weight, second_bias=second_bias)


def convolve(source, weight, bias_vec):
    frames = source.shape[0] - 2
    row_count = source.shape[1] - 2
    col_count = source.shape[2]
    padded = jnp.pad(source, ((0, 0), (0, 0), (1, 1), (0, 0)))
    summed = jnp.zeros((frames, row_count, col_count, weight.shape[-1]), jnp.float32)
    for step_t in range(3):
        for step_y in range(3):
            window = padded[step_t:step_t + frames, step_y:step_y + row_count]
            stacked = jnp.concatenate([window[:, :, step_x:step_x + col_count] for step_x in range(3)], axis=-1)
            summed = summed + jnp.einsum('abcd,de->abce', stacked.astype(jnp.float32), weight[step_t, step_y].astype(jnp.float32))
    return summed + bias_vec

def norm_silu(values, gain_vec):
    values = values.astype(jnp.float32)
    scaled = values * lax.rsqrt(lax.optimization_barrier(jnp.mean(values * values, axis=-1, keepdims=True)) + 1e-06)
    return jax.nn.silu(scaled * gain_vec).astype(jnp.bfloat16)

def pad_edges(frames_block):
    return jnp.pad(frames_block, ((2, 0), (1, 1), (0, 0), (0, 0)))

def reference(latent, routing, counts, offsets, in_weight, in_bias, first_gain, first_weight, first_bias, second_gain, second_weight, second_bias):
    frame_total = SPANS * FR
    span_of = jnp.arange(frame_total, dtype=jnp.int32) // FR

    def decode(video_index):
        frames_in = latent[:, :, video_index].reshape(frame_total, WROWS, COLS, Z)
        live_mask = ((span_of >= offsets[video_index]) & (span_of < offsets[video_index] + counts[video_index])).astype(jnp.float32)[:, None, None, None]
        latent_frames = (frames_in * live_mask).astype(jnp.bfloat16)
        hidden = (convolve(pad_edges(latent_frames), in_weight, in_bias) * live_mask).astype(jnp.bfloat16)
        middle = convolve(pad_edges(norm_silu(hidden, first_gain)), first_weight, first_bias) * live_mask
        result = convolve(pad_edges(norm_silu(middle, second_gain)), second_weight, second_bias)
        return ((result + hidden.astype(jnp.float32)) * live_mask).astype(jnp.bfloat16)
    decoded = lax.map(decode, jnp.arange(VIDS, dtype=jnp.int32))
    placed = jnp.zeros_like(decoded).at[routing].set(decoded)
    group_count = VIDS // VPG
    placed = placed.reshape(group_count, VPG, SPANS, FR, BANDS, ROWS, COLS, C)
    placed = jnp.transpose(placed, (2, 3, 0, 4, 1, 5, 6, 7)).reshape(SPANS, FR, VIDS * WROWS, COLS, C)
    return jnp.roll(placed, -(BANDS // 2) * VPG * ROWS, axis=2)
```

```python
import functools

import jax
import jax.numpy as jnp
from jax import lax
from jax.experimental import pallas as pl
from jax.experimental.pallas import tpu as pltpu
from jax.sharding import PartitionSpec as P

BANDS = 4
VPG = 2
F32 = jnp.float32
BF16 = jnp.bfloat16
LIMIT = 58 * 1024 * 1024


def weight_copies(weight_ref, held, sems):
    width = weight_ref.shape[-1]
    return [
        pltpu.make_async_copy(
            weight_ref.at[i, j], held.at[j, :, pl.ds(i * width, width)], sems.at[i, j]
        )
        for j in range(3)
        for i in range(3)
    ]


def spread_columns(values, cols):
    rows = values.shape[0]
    place = lax.broadcasted_iota(jnp.int32, values.shape, 0) % cols
    left = jnp.where(place == 0, 0.0, pltpu.roll(values, 1, 0))
    right = jnp.where(place == cols - 1, 0.0, pltpu.roll(values, rows - 1, 0))
    return jnp.concatenate(
        [left.astype(BF16), values.astype(BF16), right.astype(BF16)], axis=-1
    )


def norm_silu(values, gain):
    scale = lax.rsqrt(jnp.mean(values * values, axis=-1, keepdims=True) + 1e-06)
    half = (0.5 * gain) * (values * scale)
    return half + half * jnp.tanh(half)


def accumulate(acc, x, w):
    width = acc.shape[-1]
    rows = acc.shape[1]
    frames = acc.shape[0]

    def step(j, carry):
        for a in range(frames + 2):
            low, high = max(0, a - frames + 1), min(2, a)
            lhs = x[a, pl.ds(j, 3)].reshape(rows, 3 * width)
            res = jnp.dot(
                lhs, w[j, :, low * width : (high + 1) * width], preferred_element_type=F32
            )
            for i in range(low, high + 1):
                acc[a - i] += res[:, (i - low) * width : (i - low + 1) * width]
        return carry

    lax.fori_loop(0, 3, step, 0)


def video_scale(mask_ref, frame, half):
    place = lax.broadcasted_iota(jnp.int32, (half * VPG, 1), 0)
    return jnp.where(place < half, mask_ref[frame, 0], mask_ref[frame, 1])


def front_kernel(
    live_ref, keep_ref, lat_ref, in_w_ref, in_b_ref, gain1_ref, b1_ref, gain2_ref, w1_ref,
    hidden_ref, second_ref, x, w, acc, sems,
):
    width = in_w_ref.shape[-1]
    lanes = lat_ref.shape[-1]
    cols = lanes // VPG
    copies = weight_copies(w1_ref, w, sems)
    for copy in copies:
        copy.start()
    frames, rows = x.shape[0], x.shape[1]

    def cell(index, carry):
        f, r = index // rows, index % rows
        taps = jnp.concatenate(
            [lat_ref[f + i, r + j] for i in range(3) for j in range(3)], axis=0
        )
        value = lax.dot_general(
            taps, in_w_ref[...], (((0,), (0,)), ((), ())), preferred_element_type=F32
        )
        scale = video_scale(live_ref, f, cols) * keep_ref[r]
        value = ((value + in_b_ref[...]) * scale).astype(BF16)
        hidden_ref[f, r] = value
        x[f, r] = spread_columns(norm_silu(value.astype(F32), gain1_ref[...]), cols)
        return carry

    lax.fori_loop(0, frames * rows, cell, 0)
    for o in range(acc.shape[0]):
        acc[o] = jnp.broadcast_to(b1_ref[...], acc.shape[1:])
    for copy in copies:
        copy.wait()
    accumulate(acc, x, w)

    def finish(index, carry):
        f, r = index // (rows - 2), index % (rows - 2)
        value = acc[f, pl.ds(pl.multiple_of(r * lanes, lanes), lanes)]
        value = value * video_scale(live_ref, f + 2, cols)
        second_ref[f, r] = norm_silu(value, gain2_ref[...]).astype(BF16)
        return carry

    lax.fori_loop(0, acc.shape[0] * (rows - 2), finish, 0)


def back_kernel(
    live_ref, keep_ref, own_ref, behind_ref, above_ref, below_ref, hidden_ref, b2_ref, w2_ref,
    out_ref, x, w, acc, sems,
):
    frames, rows, lanes, width = own_ref.shape
    cols = lanes // VPG
    copies = weight_copies(w2_ref, w, sems)
    for copy in copies:
        copy.start()

    def fill_own(index, carry):
        f, r = index // rows, index % rows
        x[f + 2, r + 1] = spread_columns(own_ref[f, r].astype(F32), cols)
        return carry

    lax.fori_loop(0, frames * rows, fill_own, 0)

    def fill_behind(index, carry):
        f, r = index // rows, index % rows
        x[f, r + 1] = spread_columns(behind_ref[f, r].astype(F32), cols)
        return carry

    lax.fori_loop(0, 2 * rows, fill_behind, 0)

    def fill_rows(f, carry):
        x[f, 0] = spread_columns(above_ref[f].astype(F32) * keep_ref[0], cols)
        x[f, rows + 1] = spread_columns(below_ref[f].astype(F32) * keep_ref[rows + 1], cols)
        return carry

    lax.fori_loop(0, frames + 2, fill_rows, 0)
    for o in range(frames):
        acc[o] = jnp.broadcast_to(b2_ref[...], acc.shape[1:])
    for copy in copies:
        copy.wait()
    accumulate(acc, x, w)

    for f in range(frames):
        for r in range(rows):
            value = acc[f, r * lanes : (r + 1) * lanes] + hidden_ref[f + 2, r + 1].astype(F32)
            value = (value * video_scale(live_ref, f + 2, cols)).astype(BF16)
            for v in range(VPG):
                out_ref[f, v * rows + r] = value[v * cols : (v + 1) * cols]


def on_device(
    latent, routing, counts, offsets, in_weight, in_bias, first_gain, first_weight, first_bias,
    second_gain, second_weight, second_bias,
):
    groups = lax.axis_size("video")
    spans = lax.axis_size("tm")
    group_count = groups // BANDS
    _, frames, videos, window_rows, local_cols, z = latent.shape
    rows = window_rows // BANDS
    width = in_weight.shape[-1]
    cols = local_cols * groups
    lanes = VPG * cols
    device_index = lax.axis_index("video")
    placed = (device_index + BANDS // 2) % groups
    group, band = placed // BANDS, placed % BANDS
    span = lax.axis_index("tm")

    slots = jnp.arange(videos, dtype=jnp.int32)
    chosen = routing[:, None] == slots[None, :]
    video_of = jnp.sum(jnp.where(chosen, slots[:, None], 0), axis=0)
    first_span = jnp.sum(jnp.where(chosen, offsets[:, None], 0), axis=0)
    last_span = first_span + jnp.sum(jnp.where(chosen, counts[:, None], 0), axis=0)
    first_own = lax.dynamic_slice_in_dim(first_span, group * VPG, VPG)
    last_own = lax.dynamic_slice_in_dim(last_span, group * VPG, VPG)
    relative = jnp.arange(frames + 4, dtype=jnp.int32) - 4
    span_of = span + jnp.floor_divide(relative, frames)
    live = ((span_of[:, None] >= first_own) & (span_of[:, None] < last_own)).astype(F32)
    row_ids = band * rows - 1 + jnp.arange(rows + 2, dtype=jnp.int32)
    keep = ((row_ids >= 0) & (row_ids < window_rows)).astype(F32)

    own = jnp.take(latent[0], video_of, axis=1)
    one = lax.ppermute(own, "tm", [(i, i + 1) for i in range(spans - 1)])
    two = lax.ppermute(own[-1:], "tm", [(i, i + 2) for i in range(spans - 2)])
    line = jnp.concatenate([two, one, own], axis=0)
    line = jnp.pad(line, ((0, 0), (0, 0), (2, 2), (0, 0), (0, 0)))
    bands = jnp.stack(
        [line[:, :, b * rows : b * rows + rows + 4] for b in range(BANDS)], axis=0
    )
    bands = bands.reshape(BANDS, frames + 4, group_count, VPG, rows + 4, local_cols, z)
    bands = jnp.transpose(bands, (2, 0, 1, 4, 3, 6, 5))
    bands = bands.reshape(groups, frames + 4, rows + 4, VPG, z, local_cols)
    bands = jnp.roll(bands, -(BANDS // 2), axis=0)
    came = lax.all_to_all(bands, "video", split_axis=0, concat_axis=0, tiled=True)
    came = jnp.transpose(came, (1, 2, 4, 3, 0, 5)).reshape(frames + 4, rows + 4, z, VPG, cols)
    came = (came * live[:, None, None, :, None]).astype(BF16)
    wide = jnp.pad(came, ((0, 0),) * 4 + ((1, 1),))
    stacked = jnp.stack([wide[..., k : k + cols] for k in range(3)], axis=2)
    stacked = stacked.reshape(frames + 4, rows + 4, 3 * z, lanes)

    vmem = pl.BlockSpec(memory_space=pltpu.VMEM)
    smem = pl.BlockSpec(memory_space=pltpu.SMEM)
    hbm = pl.BlockSpec(memory_space=pl.ANY)
    scratch = [
        pltpu.VMEM((frames + 2, rows + 2, lanes, 3 * width), BF16),
        pltpu.VMEM((3, 3 * width, 3 * width), BF16),
        pltpu.VMEM((frames, rows * lanes, width), F32),
        pltpu.SemaphoreType.DMA((3, 3)),
    ]
    params = pltpu.CompilerParams(vmem_limit_bytes=LIMIT)
    live5 = live[2:]
    hidden, second = pl.pallas_call(
        front_kernel,
        out_shape=(
            jax.ShapeDtypeStruct((frames + 2, rows + 2, lanes, width), BF16),
            jax.ShapeDtypeStruct((frames, rows, lanes, width), BF16),
        ),
        in_specs=[smem, smem] + [vmem] * 6 + [hbm],
        out_specs=(vmem, vmem),
        scratch_shapes=scratch,
        compiler_params=params,
    )(
        live5, keep, stacked, in_weight.reshape(9 * 3 * z, width), in_bias[None],
        first_gain[None], first_bias[None], second_gain[None], first_weight,
    )

    behind = lax.ppermute(second[-2:], "tm", [(i, i + 1) for i in range(spans - 1)])
    tall = jnp.concatenate([behind[:, 0::rows - 1], second[:, 0::rows - 1]], axis=0)
    above = lax.ppermute(
        tall[:, 1], "video", [(i, (i + 1) % groups) for i in range(groups)]
    )
    below = lax.ppermute(
        tall[:, 0], "video", [((i + 1) % groups, i) for i in range(groups)]
    )
    out = pl.pallas_call(
        back_kernel,
        out_shape=jax.ShapeDtypeStruct((frames, VPG * rows, cols, width), BF16),
        in_specs=[smem, smem] + [vmem] * 6 + [hbm],
        out_specs=vmem,
        scratch_shapes=scratch,
        compiler_params=params,
    )(live5, keep, second, behind, above, below, hidden, second_bias[None], second_weight)
    return out[None]


def solution(mesh):
    in_specs = (P("tm", None, None, None, "video", None),) + (P(),) * 11
    return jax.shard_map(
        on_device,
        mesh=mesh,
        in_specs=in_specs,
        out_specs=P("tm", None, "video", None, None),
        check_vma=False,
    )
```

```python
import functools

import jax
import jax.numpy as jnp
from jax import lax
from jax.experimental import pallas as pl
from jax.experimental.pallas import tpu as pltpu
from jax.sharding import PartitionSpec as P

BANDS = 4
VPG = 2
F32 = jnp.float32
BF16 = jnp.bfloat16
LIMIT = 58 * 1024 * 1024


def weight_copies(weight_ref, held, sems):
    width = weight_ref.shape[-1]
    return [
        pltpu.make_async_copy(
            weight_ref.at[i, j], held.at[j, :, pl.ds(i * width, width)], sems.at[i, j]
        )
        for j in range(3)
        for i in range(3)
    ]


def spread_columns(place, values, tile):
    rows, width = values.shape
    held = values.astype(BF16)
    which = lax.broadcasted_iota(jnp.int32, (tile, width), 0)
    first = pltpu.roll(values[rows - tile :], VPG, 0)
    last = pltpu.roll(values[:tile], tile - VPG, 0)
    place[:tile, :width] = jnp.where(which < VPG, 0.0, first).astype(BF16)
    place[tile:, :width] = held[: rows - tile]
    place[:, width : 2 * width] = held
    place[: rows - tile, 2 * width :] = held[tile:]
    place[rows - tile :, 2 * width :] = jnp.where(which >= tile - VPG, 0.0, last).astype(BF16)


def norm_silu(values, gain):
    scale = lax.rsqrt(jnp.mean(values * values, axis=-1, keepdims=True) + 1e-06)
    half = (0.5 * gain) * (values * scale)
    return half + half * jnp.tanh(half)


def accumulate(acc, x, w):
    width = acc.shape[-1]
    rows = acc.shape[1]
    frames = acc.shape[0]

    def step(j, carry):
        for a in range(frames + 2):
            low, high = max(0, a - frames + 1), min(2, a)
            lhs = x[a, pl.ds(j, 3)].reshape(rows, 3 * width)
            res = jnp.dot(
                lhs, w[j, :, low * width : (high + 1) * width], preferred_element_type=F32
            )
            for i in range(low, high + 1):
                acc[a - i] += res[:, (i - low) * width : (i - low + 1) * width]
        return carry

    lax.fori_loop(0, 3, step, 0)


def video_scale(mask_ref, frame, lanes):
    place = lax.broadcasted_iota(jnp.int32, (lanes, 1), 0)
    return jnp.where(place % VPG == 0, mask_ref[frame, 0], mask_ref[frame, 1])


def gather_taps(lat_ref, q, z, blocks):
    tile = lat_ref.shape[2]
    rows = q.shape[1]

    def frame(f, carry):
        near = [lat_ref[f, r].astype(F32) for r in range(rows + 2)]
        for c in range(blocks):
            cut = [value[:, c * z : c * z + 64] for value in near]
            blank = jnp.zeros((tile, 64), F32)
            for r in range(rows):
                both = jnp.concatenate([cut[r], cut[r + 1], cut[r + 2], blank], axis=1)
                q[f, r, c * tile : (c + 1) * tile] = both.astype(BF16)
        return carry

    lax.fori_loop(0, lat_ref.shape[0], frame, 0)


def front_kernel(
    live_ref, keep_ref, lat_ref, in_w_ref, in_b_ref, gain1_ref, b1_ref, gain2_ref, w1_ref,
    hidden_ref, second_ref, x, w, acc, sems, q, *, z,
):
    copies = weight_copies(w1_ref, w, sems)
    for copy in copies:
        copy.start()
    frames, rows, lanes = x.shape[:3]
    tile = lat_ref.shape[2]
    gather_taps(lat_ref, q, z, lanes // tile)

    def cell(index, carry):
        f, r = index // rows, index % rows
        taps = jnp.concatenate([q[f + i, r] for i in range(3)], axis=1)
        value = jnp.dot(taps, in_w_ref[...], preferred_element_type=F32)
        scale = video_scale(live_ref, f, lanes) * keep_ref[r]
        value = ((value + in_b_ref[...]) * scale).astype(BF16)
        hidden_ref[f, r] = value
        spread_columns(x.at[f, r], norm_silu(value.astype(F32), gain1_ref[...]), tile)
        return carry

    lax.fori_loop(0, frames * rows, cell, 0)
    for o in range(acc.shape[0]):
        acc[o] = jnp.broadcast_to(b1_ref[...], acc.shape[1:])
    for copy in copies:
        copy.wait()
    accumulate(acc, x, w)

    def finish(index, carry):
        f, r = index // (rows - 2), index % (rows - 2)
        value = acc[f, pl.ds(pl.multiple_of(r * lanes, lanes), lanes)]
        value = value * video_scale(live_ref, f + 2, lanes)
        second_ref[f, r] = norm_silu(value, gain2_ref[...]).astype(BF16)
        return carry

    lax.fori_loop(0, acc.shape[0] * (rows - 2), finish, 0)


def back_kernel(
    live_ref, keep_ref, own_ref, behind_ref, above_ref, below_ref, hidden_ref, b2_ref, w2_ref,
    out_ref, x, w, acc, sems, turn, *, tile,
):
    frames, rows, lanes, width = own_ref.shape
    copies = weight_copies(w2_ref, w, sems)
    for copy in copies:
        copy.start()

    def fill_own(index, carry):
        f, r = index // rows, index % rows
        spread_columns(x.at[f + 2, r + 1], own_ref[f, r].astype(F32), tile)
        return carry

    lax.fori_loop(0, frames * rows, fill_own, 0)

    def fill_behind(index, carry):
        f, r = index // rows, index % rows
        spread_columns(x.at[f, r + 1], behind_ref[f, r].astype(F32), tile)
        return carry

    lax.fori_loop(0, 2 * rows, fill_behind, 0)

    def fill_rows(f, carry):
        spread_columns(x.at[f, 0], above_ref[f].astype(F32) * keep_ref[0], tile)
        spread_columns(x.at[f, rows + 1], below_ref[f].astype(F32) * keep_ref[rows + 1], tile)
        return carry

    lax.fori_loop(0, frames + 2, fill_rows, 0)
    for o in range(frames):
        acc[o] = jnp.broadcast_to(b2_ref[...], acc.shape[1:])
    for copy in copies:
        copy.wait()
    accumulate(acc, x, w)

    blocks = lanes // tile
    parts = width // 128
    for f in range(frames):
        for r in range(rows):
            value = acc[f, r * lanes : (r + 1) * lanes] + hidden_ref[f + 2, r + 1].astype(F32)
            value = value * video_scale(live_ref, f + 2, lanes)
            for k in range(parts):
                turn[k] = value[:, k * 128 : (k + 1) * 128]
            for v in range(VPG):
                for k in range(parts):
                    line = [
                        turn[k, pl.ds(s * VPG + v, blocks, stride=tile)]
                        for s in range(tile // VPG)
                    ]
                    line = jnp.concatenate(line, axis=0).astype(BF16)
                    out_ref[f, v * rows + r, :, k * 128 : (k + 1) * 128] = line


def on_device(
    latent, routing, counts, offsets, in_weight, in_bias, first_gain, first_weight, first_bias,
    second_gain, second_weight, second_bias,
):
    groups = lax.axis_size("video")
    spans = lax.axis_size("tm")
    group_count = groups // BANDS
    _, frames, videos, window_rows, local_cols, z = latent.shape
    rows = window_rows // BANDS
    width = in_weight.shape[-1]
    cols = local_cols * groups
    lanes = VPG * cols
    device_index = lax.axis_index("video")
    placed = (device_index + BANDS // 2) % groups
    group, band = placed // BANDS, placed % BANDS
    span = lax.axis_index("tm")

    slots = jnp.arange(videos, dtype=jnp.int32)
    chosen = routing[:, None] == slots[None, :]
    video_of = jnp.sum(jnp.where(chosen, slots[:, None], 0), axis=0)
    first_span = jnp.sum(jnp.where(chosen, offsets[:, None], 0), axis=0)
    last_span = first_span + jnp.sum(jnp.where(chosen, counts[:, None], 0), axis=0)
    first_own = lax.dynamic_slice_in_dim(first_span, group * VPG, VPG)
    last_own = lax.dynamic_slice_in_dim(last_span, group * VPG, VPG)
    relative = jnp.arange(frames + 4, dtype=jnp.int32) - 4
    span_of = span + jnp.floor_divide(relative, frames)
    live = ((span_of[:, None] >= first_own) & (span_of[:, None] < last_own)).astype(F32)
    row_ids = band * rows - 1 + jnp.arange(rows + 2, dtype=jnp.int32)
    keep = ((row_ids >= 0) & (row_ids < window_rows)).astype(F32)

    flat = latent[0].reshape(frames, videos, window_rows, local_cols * z)
    own = jnp.take(flat, video_of, axis=1)
    one = lax.ppermute(own, "tm", [(i, i + 1) for i in range(spans - 1)])
    two = lax.ppermute(own[-1:], "tm", [(i, i + 2) for i in range(spans - 2)])
    line = jnp.concatenate([two, one, own], axis=0)
    line = jnp.pad(line, ((0, 0), (0, 0), (2, 2), (0, 0)))
    bands = jnp.stack(
        [line[:, :, b * rows : b * rows + rows + 4] for b in range(BANDS)], axis=0
    )
    bands = bands.reshape(BANDS, frames + 4, group_count, VPG, rows + 4, local_cols * z)
    bands = jnp.transpose(bands, (2, 0, 1, 4, 3, 5))
    bands = bands.reshape(groups, frames + 4, rows + 4, VPG, local_cols * z)
    bands = jnp.roll(bands, -(BANDS // 2), axis=0)
    came = lax.all_to_all(bands, "video", split_axis=0, concat_axis=0, tiled=True)
    came = jnp.transpose(came, (1, 2, 0, 3, 4))
    came = (came * live[:, None, None, :, None]).astype(BF16)
    behind = jnp.pad(came[:, :, :-1, :, -z:], ((0, 0), (0, 0), (1, 0), (0, 0), (0, 0)))
    ahead = jnp.pad(came[:, :, 1:, :, :z], ((0, 0), (0, 0), (0, 1), (0, 0), (0, 0)))
    spare = jnp.zeros(came.shape[:4] + (-(local_cols + 2) * z % 128,), BF16)
    stacked = jnp.concatenate([behind, came, ahead, spare], axis=-1)
    tile = groups * VPG
    stacked = stacked.reshape(frames + 4, rows + 4, tile, -1)
    taps = jnp.pad(
        in_weight.reshape(3, 3, 3 * z, width), ((0, 0), (0, 1), (0, 64 - 3 * z), (0, 0))
    ).reshape(3 * 4 * 64, width)

    vmem = pl.BlockSpec(memory_space=pltpu.VMEM)
    smem = pl.BlockSpec(memory_space=pltpu.SMEM)
    hbm = pl.BlockSpec(memory_space=pl.ANY)
    scratch = [
        pltpu.VMEM((frames + 2, rows + 2, lanes, 3 * width), BF16),
        pltpu.VMEM((3, 3 * width, 3 * width), BF16),
        pltpu.VMEM((frames, rows * lanes, width), F32),
        pltpu.SemaphoreType.DMA((3, 3)),
    ]
    params = pltpu.CompilerParams(vmem_limit_bytes=LIMIT)
    live5 = live[2:]
    hidden, second = pl.pallas_call(
        functools.partial(front_kernel, z=z),
        out_shape=(
            jax.ShapeDtypeStruct((frames + 2, rows + 2, lanes, width), BF16),
            jax.ShapeDtypeStruct((frames, rows, lanes, width), BF16),
        ),
        in_specs=[smem, smem] + [vmem] * 6 + [hbm],
        out_specs=(vmem, vmem),
        scratch_shapes=scratch
        + [pltpu.VMEM((frames + 4, rows + 2, lanes, 256), BF16)],
        compiler_params=params,
    )(
        live5, keep, stacked, taps, in_bias[None],
        first_gain[None], first_bias[None], second_gain[None], first_weight,
    )

    behind = lax.ppermute(second[-2:], "tm", [(i, i + 1) for i in range(spans - 1)])
    tall = jnp.concatenate([behind[:, 0::rows - 1], second[:, 0::rows - 1]], axis=0)
    above = lax.ppermute(
        tall[:, 1], "video", [(i, (i + 1) % groups) for i in range(groups)]
    )
    below = lax.ppermute(
        tall[:, 0], "video", [((i + 1) % groups, i) for i in range(groups)]
    )
    out = pl.pallas_call(
        functools.partial(back_kernel, tile=tile),
        out_shape=jax.ShapeDtypeStruct((frames, VPG * rows, cols, width), BF16),
        in_specs=[smem, smem] + [vmem] * 6 + [hbm],
        out_specs=vmem,
        scratch_shapes=scratch + [pltpu.VMEM((width // 128, lanes, 128), F32)],
        compiler_params=params,
    )(live5, keep, second, behind, above, below, hidden, second_bias[None], second_weight)
    return out[None]


def solution(mesh):
    in_specs = (P("tm", None, None, None, "video", None),) + (P(),) * 11
    return jax.shard_map(
        on_device,
        mesh=mesh,
        in_specs=in_specs,
        out_specs=P("tm", None, "video", None, None),
        check_vma=False,
    )
```

```python
import functools

import jax
import jax.numpy as jnp
from jax import lax
from jax.experimental import pallas as pl
from jax.experimental.pallas import tpu as pltpu
from jax.sharding import PartitionSpec as P

BANDS = 4
VPG = 2
F32 = jnp.float32
BF16 = jnp.bfloat16
LIMIT = 58 * 1024 * 1024


def weight_copies(weight_ref, held, sems):
    width = weight_ref.shape[-1]
    return [
        pltpu.make_async_copy(
            weight_ref.at[i, j], held.at[j, :, pl.ds(i * width, width)], sems.at[i, j]
        )
        for j in range(3)
        for i in range(3)
    ]


def spread_columns(place, values, tile):
    rows, width = values.shape
    held = values.astype(BF16)
    which = lax.broadcasted_iota(jnp.int32, (tile, width), 0)
    first = pltpu.roll(values[rows - tile :], VPG, 0)
    last = pltpu.roll(values[:tile], tile - VPG, 0)
    place[:tile, :width] = jnp.where(which < VPG, 0.0, first).astype(BF16)
    place[tile:, :width] = held[: rows - tile]
    place[:, width : 2 * width] = held
    place[: rows - tile, 2 * width :] = held[tile:]
    place[rows - tile :, 2 * width :] = jnp.where(which >= tile - VPG, 0.0, last).astype(BF16)


def norm_silu(values, gain):
    scale = lax.rsqrt(jnp.mean(values * values, axis=-1, keepdims=True) + 1e-06)
    half = (0.5 * gain) * (values * scale)
    return half + half * jnp.tanh(half)


def accumulate(acc, x, w, outs, ins, part):
    width = acc.shape[-1]
    lanes = x.shape[2]
    steps, (tap, tap_by), (row, row_by), count = part

    def step(t, carry):
        j, first = tap + t * tap_by, row + t * row_by
        cells = pl.ds(pl.multiple_of((first - j) * lanes, lanes), count * lanes)
        for a in ins:
            low, high = max(0, a - outs[-1]), min(2, a - outs[0])
            lhs = x[a, pl.ds(first, count)].reshape(count * lanes, 3 * width)
            res = jnp.dot(
                lhs, w[j, :, low * width : (high + 1) * width], preferred_element_type=F32
            )
            for i in range(low, high + 1):
                acc[a - i, cells] += res[:, (i - low) * width : (i - low + 1) * width]
        return carry

    lax.fori_loop(0, steps, step, 0)


def video_scale(mask_ref, frame, lanes):
    place = lax.broadcasted_iota(jnp.int32, (lanes, 1), 0)
    return jnp.where(place % VPG == 0, mask_ref[frame, 0], mask_ref[frame, 1])


def gather_taps(lat_ref, q, z, blocks):
    tile = lat_ref.shape[2]
    rows = q.shape[1]

    def frame(f, carry):
        near = [lat_ref[f, r].astype(F32) for r in range(rows + 2)]
        for c in range(blocks):
            cut = [value[:, c * z : c * z + 64] for value in near]
            blank = jnp.zeros((tile, 64), F32)
            for r in range(rows):
                both = jnp.concatenate([cut[r], cut[r + 1], cut[r + 2], blank], axis=1)
                q[f, r, c * tile : (c + 1) * tile] = both.astype(BF16)
        return carry

    lax.fori_loop(0, lat_ref.shape[0], frame, 0)


def block_kernel(
    live_ref, keep_ref, lat_ref, in_w_ref, in_b_ref, gain1_ref, b1_ref, gain2_ref, b2_ref,
    w1_ref, w2_ref, out_ref,
    x, w1, w2, acc, q, hidden, second, behind, above, below, turn,
    w1_sems, w2_sems, send_sems, recv_sems, *, z, spans, groups,
):
    span, place = lax.axis_index("tm"), lax.axis_index("video")
    band = (place + BANDS // 2) % groups % BANDS
    up, down = (place + 1) % groups, (place + groups - 1) % groups
    first, last = span == 0, span == spans - 1
    top, bottom = band == 0, band == BANDS - 1
    ways = [
        (jnp.logical_not(first), {"tm": span - 1}),
        (jnp.logical_not(last), {"tm": span + 1}),
        (jnp.logical_not(top), {"video": down}),
        (jnp.logical_not(bottom), {"video": up}),
    ]
    barrier = pltpu.get_barrier_semaphore()
    for there, device in ways:
        @pl.when(there)
        def _(device=device):
            pl.semaphore_signal(
                barrier, inc=1, device_id=device, device_id_type=pl.DeviceIdType.MESH
            )

    loads = weight_copies(w1_ref, w1, w1_sems)
    more_loads = weight_copies(w2_ref, w2, w2_sems)
    for copy in loads:
        copy.start()
    frames, rows = second.shape[:2]
    lanes, tile = x.shape[2], lat_ref.shape[2]

    def remote(source, target, k, device):
        return pltpu.make_async_remote_copy(
            src_ref=source, dst_ref=target, send_sem=send_sems.at[k], recv_sem=recv_sems.at[k],
            device_id=device, device_id_type=pl.DeviceIdType.MESH,
        )

    late, early = pl.ds(frames - 2, 2), pl.ds(0, frames - 2)
    back = remote(second.at[late], behind, 0, {"tm": span + 1})
    to_up = [
        remote(second.at[late, rows - 1], above.at[pl.ds(frames, 2)], 1, {"video": up}),
        remote(second.at[early, rows - 1], above.at[pl.ds(2, frames - 2)], 2, {"video": up}),
        remote(behind.at[:, rows - 1], above.at[pl.ds(0, 2)], 3, {"video": up}),
    ]
    to_down = [
        remote(second.at[late, 0], below.at[pl.ds(frames, 2)], 4, {"video": down}),
        remote(second.at[early, 0], below.at[pl.ds(2, frames - 2)], 5, {"video": down}),
        remote(behind.at[:, 0], below.at[pl.ds(0, 2)], 6, {"video": down}),
    ]

    def send_rows(k):
        @pl.when(jnp.logical_not(bottom))
        def _():
            to_up[k].start()

        @pl.when(jnp.logical_not(top))
        def _():
            to_down[k].start()

    gather_taps(lat_ref, q, z, lanes // tile)

    def cell(index, carry):
        f, r = index // (rows + 2), index % (rows + 2)
        taps = jnp.concatenate([q[f + i, r] for i in range(3)], axis=1)
        value = jnp.dot(taps, in_w_ref[...], preferred_element_type=F32)
        scale = video_scale(live_ref, f, lanes) * keep_ref[r]
        value = ((value + in_b_ref[...]) * scale).astype(BF16)
        hidden[f, r] = value
        spread_columns(x.at[f, r], norm_silu(value.astype(F32), gain1_ref[...]), tile)
        return carry

    lax.fori_loop(0, (frames + 2) * (rows + 2), cell, 0)
    for o in range(frames):
        acc[o] = jnp.broadcast_to(b1_ref[...], acc.shape[1:])
    for copy in loads:
        copy.wait()
    for copy in more_loads:
        copy.start()
    whole = (3, (0, 1), (0, 1), rows)

    def finish(f):
        def row(r, carry):
            value = acc[f, pl.ds(pl.multiple_of(r * lanes, lanes), lanes)]
            value = value * video_scale(live_ref, f + 2, lanes)
            second[f, r] = norm_silu(value, gain2_ref[...]).astype(BF16)
            return carry

        lax.fori_loop(0, rows, row, 0)

    accumulate(acc, x, w1, range(frames - 2, frames), range(frames - 2, frames + 2), whole)
    for f in range(frames - 2, frames):
        finish(f)
    pl.semaphore_wait(barrier, sum(jnp.where(there, 1, 0) for there, _ in ways))

    @pl.when(jnp.logical_not(last))
    def _():
        back.start()

    send_rows(0)
    accumulate(acc, x, w1, range(0, frames - 2), range(0, frames), whole)
    for f in range(frames - 2):
        finish(f)
    send_rows(1)

    def fill(source, at_frame, at_row, count):
        def one(index, carry):
            f, r = index // rows, index % rows
            spread_columns(x.at[f + at_frame, r + at_row], source[f, r].astype(F32), tile)
            return carry

        lax.fori_loop(0, count * rows, one, 0)

    def fill_edges(start, count, ks):
        for source, empty, copies, at_row in (
            (above, top, to_up, 0), (below, bottom, to_down, rows + 1)
        ):
            @pl.when(jnp.logical_not(empty))
            def _(source=source, copies=copies, at_row=at_row):
                for k in ks:
                    copies[k].wait_recv()

                def one(f, carry):
                    spread_columns(x.at[f, at_row], source[f].astype(F32), tile)
                    return carry

                lax.fori_loop(start, start + count, one, 0)

            @pl.when(empty)
            def _(at_row=at_row):
                for f in range(start, start + count):
                    x[f, at_row] = jnp.zeros(x.shape[2:], BF16)

    fill(second, 2, 1, frames)
    for o in range(frames):
        acc[o] = jnp.broadcast_to(b2_ref[...], acc.shape[1:])
    for copy in more_loads:
        copy.wait()
    own_frames, every = range(2, frames + 2), range(frames)
    middle = (1, (1, 0), (1, 0), rows)
    beside = (2, (0, 2), (1, 1), rows - 1)
    outer = (2, (0, 2), (0, rows + 1), 1)
    accumulate(acc, x, w2, every, own_frames, middle)
    accumulate(acc, x, w2, every, own_frames, beside)
    fill_edges(2, frames, (0, 1))
    accumulate(acc, x, w2, every, own_frames, outer)

    @pl.when(jnp.logical_not(first))
    def _():
        back.wait_recv()

    @pl.when(first)
    def _():
        behind[...] = jnp.zeros(behind.shape, BF16)

    send_rows(2)
    fill(behind, 0, 1, 2)
    accumulate(acc, x, w2, every, range(2), middle)
    accumulate(acc, x, w2, every, range(2), beside)
    fill_edges(0, 2, (2,))
    accumulate(acc, x, w2, every, range(2), outer)

    blocks = lanes // tile
    for f in range(frames):
        for r in range(rows):
            value = acc[f, r * lanes : (r + 1) * lanes] + hidden[f + 2, r + 1].astype(F32)
            value = value * video_scale(live_ref, f + 2, lanes)
            for k in range(turn.shape[0]):
                turn[k] = value[:, k * 128 : (k + 1) * 128]
            for v in range(VPG):
                for k in range(turn.shape[0]):
                    line = [
                        turn[k, pl.ds(s * VPG + v, blocks, stride=tile)]
                        for s in range(tile // VPG)
                    ]
                    line = jnp.concatenate(line, axis=0).astype(BF16)
                    out_ref[f, v * rows + r, :, k * 128 : (k + 1) * 128] = line

    @pl.when(jnp.logical_not(last))
    def _():
        back.wait_send()

    for copies, empty in ((to_up, bottom), (to_down, top)):
        @pl.when(jnp.logical_not(empty))
        def _(copies=copies):
            for copy in copies:
                copy.wait_send()


def on_device(
    latent, routing, counts, offsets, in_weight, in_bias, first_gain, first_weight, first_bias,
    second_gain, second_weight, second_bias,
):
    groups = lax.axis_size("video")
    spans = lax.axis_size("tm")
    group_count = groups // BANDS
    _, frames, videos, window_rows, local_cols, z = latent.shape
    rows = window_rows // BANDS
    width = in_weight.shape[-1]
    cols = local_cols * groups
    lanes = VPG * cols
    device_index = lax.axis_index("video")
    placed = (device_index + BANDS // 2) % groups
    group, band = placed // BANDS, placed % BANDS
    span = lax.axis_index("tm")

    slots = jnp.arange(videos, dtype=jnp.int32)
    chosen = routing[:, None] == slots[None, :]
    video_of = jnp.sum(jnp.where(chosen, slots[:, None], 0), axis=0)
    first_span = jnp.sum(jnp.where(chosen, offsets[:, None], 0), axis=0)
    last_span = first_span + jnp.sum(jnp.where(chosen, counts[:, None], 0), axis=0)
    first_own = lax.dynamic_slice_in_dim(first_span, group * VPG, VPG)
    last_own = lax.dynamic_slice_in_dim(last_span, group * VPG, VPG)
    relative = jnp.arange(frames + 4, dtype=jnp.int32) - 4
    span_of = span + jnp.floor_divide(relative, frames)
    live = ((span_of[:, None] >= first_own) & (span_of[:, None] < last_own)).astype(F32)
    row_ids = band * rows - 1 + jnp.arange(rows + 2, dtype=jnp.int32)
    keep = ((row_ids >= 0) & (row_ids < window_rows)).astype(F32)

    flat = latent[0].reshape(frames, videos, window_rows, local_cols * z)
    own = jnp.take(flat, video_of, axis=1)
    one = lax.ppermute(own, "tm", [(i, i + 1) for i in range(spans - 1)])
    two = lax.ppermute(own[-1:], "tm", [(i, i + 2) for i in range(spans - 2)])
    line = jnp.concatenate([two, one, own], axis=0)
    line = jnp.pad(line, ((0, 0), (0, 0), (2, 2), (0, 0)))
    bands = jnp.stack(
        [line[:, :, b * rows : b * rows + rows + 4] for b in range(BANDS)], axis=0
    )
    bands = bands.reshape(BANDS, frames + 4, group_count, VPG, rows + 4, local_cols * z)
    bands = jnp.transpose(bands, (2, 0, 1, 4, 3, 5))
    bands = bands.reshape(groups, frames + 4, rows + 4, VPG, local_cols * z)
    bands = jnp.roll(bands, -(BANDS // 2), axis=0)
    came = lax.all_to_all(bands, "video", split_axis=0, concat_axis=0, tiled=True)
    came = jnp.transpose(came, (1, 2, 0, 3, 4))
    came = (came * live[:, None, None, :, None]).astype(BF16)
    behind = jnp.pad(came[:, :, :-1, :, -z:], ((0, 0), (0, 0), (1, 0), (0, 0), (0, 0)))
    ahead = jnp.pad(came[:, :, 1:, :, :z], ((0, 0), (0, 0), (0, 1), (0, 0), (0, 0)))
    spare = jnp.zeros(came.shape[:4] + (-(local_cols + 2) * z % 128,), BF16)
    stacked = jnp.concatenate([behind, came, ahead, spare], axis=-1)
    tile = groups * VPG
    stacked = stacked.reshape(frames + 4, rows + 4, tile, -1)
    taps = jnp.pad(
        in_weight.reshape(3, 3, 3 * z, width), ((0, 0), (0, 1), (0, 64 - 3 * z), (0, 0))
    ).reshape(3 * 4 * 64, width)

    vmem = pl.BlockSpec(memory_space=pltpu.VMEM)
    smem = pl.BlockSpec(memory_space=pltpu.SMEM)
    hbm = pl.BlockSpec(memory_space=pl.ANY)
    scratch = [
        pltpu.VMEM((frames + 2, rows + 2, lanes, 3 * width), BF16),
        pltpu.VMEM((3, 3 * width, 3 * width), BF16),
        pltpu.VMEM((3, 3 * width, 3 * width), BF16),
        pltpu.VMEM((frames, rows * lanes, width), F32),
        pltpu.VMEM((frames + 4, rows + 2, lanes, 256), BF16),
        pltpu.VMEM((frames + 2, rows + 2, lanes, width), BF16),
        pltpu.VMEM((frames, rows, lanes, width), BF16),
        pltpu.VMEM((2, rows, lanes, width), BF16),
        pltpu.VMEM((frames + 2, lanes, width), BF16),
        pltpu.VMEM((frames + 2, lanes, width), BF16),
        pltpu.VMEM((width // 128, lanes, 128), F32),
        pltpu.SemaphoreType.DMA((3, 3)),
        pltpu.SemaphoreType.DMA((3, 3)),
        pltpu.SemaphoreType.DMA((7,)),
        pltpu.SemaphoreType.DMA((7,)),
    ]
    out = pl.pallas_call(
        functools.partial(block_kernel, z=z, spans=spans, groups=groups),
        out_shape=jax.ShapeDtypeStruct((frames, VPG * rows, cols, width), BF16),
        in_specs=[smem, smem] + [vmem] * 7 + [hbm] * 2,
        out_specs=vmem,
        scratch_shapes=scratch,
        compiler_params=pltpu.CompilerParams(
            vmem_limit_bytes=LIMIT, collective_id=0, has_side_effects=True
        ),
    )(
        live[2:], keep, stacked, taps, in_bias[None], first_gain[None], first_bias[None],
        second_gain[None], second_bias[None], first_weight, second_weight,
    )
    return out[None]


def solution(mesh):
    in_specs = (P("tm", None, None, None, "video", None),) + (P(),) * 11
    return jax.shard_map(
        on_device,
        mesh=mesh,
        in_specs=in_specs,
        out_specs=P("tm", None, "video", None, None),
        check_vma=False,
    )
```
